32 devices in a mesh: seq: 16 (over z, y, core), frame: 2 (over x).
Axes of the slice: x: 2, y: 2, z: 4, core: 2. Of those that a mesh axis runs over, the one named last changes fastest.
Arguments:
- tokens: bfloat16 [2, 32, 32, 512], P('frame', 'seq'), may hold values from -6 to 6
- row_select: bfloat16 [2, 32, 32, 64], P('frame', 'seq'), may hold values from -2 to 2
- row_decay: float32 [2, 8, 32, 32], P('frame', None, 'seq'), may hold values from -1.5 to 0, as said below
- row_gain: float32 [512], replicated, may hold values from 0.25 to 1.75
- row_skip: float32 [8], replicated, may hold values from 0.5 to 1.5
- row_in: bfloat16 [512, 512], replicated, may hold values from -0.25 to 0.25
- row_out: bfloat16 [512, 512], replicated, may hold values from -0.25 to 0.25
- col_select: bfloat16 [2, 32, 32, 64], P('frame', 'seq'), may hold values from -2 to 2
- col_decay: float32 [2, 8, 32, 32], P('frame', None, 'seq'), may hold values from -1.5 to 0, as said below
- col_gain: float32 [512], replicated, may hold values from 0.25 to 1.75
- col_skip: float32 [8], replicated, may hold values from 0.5 to 1.5
- col_in: bfloat16 [512, 512], replicated, may hold values from -0.25 to 0.25
- col_out: bfloat16 [512, 512], replicated, may hold values from -0.25 to 0.25
- cotangent: bfloat16 [2, 32, 32, 512], P('frame', 'seq'), may hold values from -6 to 6
Outputs:
- mixed: bfloat16 [2, 32, 32, 512], P('frame', 'seq')
- grad_tokens: bfloat16 [2, 32, 32, 512], P('frame', 'seq')
The draws below stay inside these ranges and needn't reach their ends.
Inputs may be any that keep to these rules, and one draw needn't show every extreme that they name: `row_decay`: every entry is below zero. `col_decay`: every entry is below zero.
All inputs are finite; a program needn't handle non-finite values.
Results may differ from the reference program's by a relative error of at most 0.013.
Values may be sent and summed in bfloat16 or wider, within the bound.
A program may use at most 128 MiB of HBM per device.

```python
import jax
import jax.numpy as jnp
from jax import lax

D = 512
SCANNER_GROUPS = 8
STATE = 32
TOK_DEV = 64
ROWS = 32
COLS = 32
N_FRAME = 2


def decay_chain(key, first_count, second_count, fast_share):
    series_extent = N_FRAME * first_count * second_count
    current_paths = jax.random.split(key, 7)
    fast_heads = jax.random.uniform(current_paths[0], (SCANNER_GROUPS, 1)) < fast_share
    slow_rate = jnp.exp(jax.random.uniform(current_paths[1], (SCANNER_GROUPS, 1), minval=jnp.log(0.05), maxval=jnp.log(0.5))) / series_extent
    fast_rate = jnp.exp(jax.random.uniform(current_paths[2], (SCANNER_GROUPS, 1), minval=jnp.log(0.03), maxval=jnp.log(0.1)))
    attention_fading_speed = jnp.where(fast_heads, fast_rate, slow_rate)
    boundary_perturbation = jax.random.uniform(current_paths[3], (SCANNER_GROUPS, series_extent), minval=0.5, maxval=1.5)
    segments = series_extent // TOK_DEV
    segment_scale = jnp.exp(jax.random.uniform(current_paths[4], (SCANNER_GROUPS, segments, 1), minval=jnp.log(0.6), maxval=jnp.log(1.6)))
    dispersion_multiplier = jnp.broadcast_to(segment_scale, (SCANNER_GROUPS, segments, TOK_DEV)).reshape(SCANNER_GROUPS, series_extent)
    sudden_placements = jax.random.randint(current_paths[5], (2,), 0, series_extent)
    sudden_penalty_amounts = jnp.log(jax.random.uniform(current_paths[6], (SCANNER_GROUPS, 2), minval=0.55, maxval=0.8))
    indicator_switches = (jnp.arange(series_extent)[None, :] == sudden_placements[:, None]).astype(jnp.float32)
    sudden_occurrences = jnp.dot(sudden_penalty_amounts, indicator_switches)
    connected_series = sudden_occurrences - attention_fading_speed * boundary_perturbation * dispersion_multiplier
    return connected_series.reshape(SCANNER_GROUPS, N_FRAME, first_count, second_count).transpose(1, 0, 2, 3).astype(jnp.float32)


def draw_row_decay(key, part):
    fast_share = 0.5
    return decay_chain(jax.random.fold_in(key, 11), ROWS, COLS, fast_share)


def draw_col_decay(key, part):
    fast_share = 0.5
    return decay_chain(jax.random.fold_in(key, 23), COLS, ROWS, fast_share)


def block_levels(own_key, shape, cuts, least, largest):
    factor_of = 1.0
    for axis_at, blocks in cuts:
        steps = jax.random.uniform(jax.random.fold_in(jax.random.fold_in(own_key, 6), axis_at), (blocks,), jnp.float32, least / len(cuts), largest / len(cuts))
        factor_of = factor_of * jnp.repeat(jnp.exp(steps), shape[axis_at] // blocks).reshape((-1,) + (1,) * (len(shape) - 1 - axis_at))
    return factor_of


def gaussian(rng, shape, spread, limit, cuts=(), held_as=jnp.bfloat16):
    level = block_levels(rng, shape, cuts, -0.22, 0.18) if cuts else 1.0
    values = jax.random.normal(rng, shape, jnp.float32) * spread * level
    return jnp.minimum(jnp.maximum(values, -limit), limit).astype(held_as)


def setup_inputs(seed: int = 0) -> dict:
    keys = jax.random.split(jax.random.key(seed), 15)
    tokens = gaussian(keys[0], (N_FRAME, ROWS, COLS, D), 1.0, 6.0, ((0, 2), (1, 16)))
    row_select = gaussian(keys[1], (N_FRAME, ROWS, COLS, 2 * STATE), 0.35, 2.0, ((0, 2), (1, 16)))
    row_decay = draw_row_decay(jax.random.fold_in(keys[14], 71), 0)
    row_gain = jnp.clip(1.0 + 0.15 * jax.random.normal(keys[3], (D,), jnp.float32), 0.25, 1.75)
    row_skip = jnp.clip(jax.random.uniform(keys[4], (SCANNER_GROUPS,), jnp.float32, 0.5, 1.5), 0.5, 1.5)
    row_in = gaussian(keys[5], (D, D), D ** -0.5, 0.25)
    row_out = gaussian(keys[6], (D, D), D ** -0.5, 0.25)
    col_select = gaussian(keys[7], (N_FRAME, COLS, ROWS, 2 * STATE), 0.35, 2.0, ((0, 2), (1, 16)))
    col_decay = draw_col_decay(jax.random.fold_in(keys[14], 71), 0)
    col_gain = jnp.clip(1.0 + 0.15 * jax.random.normal(keys[9], (D,), jnp.float32), 0.25, 1.75)
    col_skip = jnp.clip(jax.random.uniform(keys[10], (SCANNER_GROUPS,), jnp.float32, 0.5, 1.5), 0.5, 1.5)
    col_in = gaussian(keys[11], (D, D), D ** -0.5, 0.25)
    col_out = gaussian(keys[12], (D, D), D ** -0.5, 0.25)
    cotangent = gaussian(keys[13], (N_FRAME, COLS, ROWS, D), 1.0, 6.0, ((0, 2), (1, 16)))
    return dict(tokens=tokens, row_select=row_select, row_decay=row_decay, row_gain=row_gain, row_skip=row_skip, row_in=row_in, row_out=row_out, col_select=col_select, col_decay=col_decay, col_gain=col_gain, col_skip=col_skip, col_in=col_in, col_out=col_out, cotangent=cotangent)


EPSILON = 1e-05
PRECISE = lax.Precision.HIGHEST

def rounded(values):
    return lax.optimization_barrier(values.astype(jnp.bfloat16)).astype(jnp.float32)

def norm_rows(values, norm_gain):
    floats = values.astype(jnp.float32)
    factor = lax.rsqrt(lax.optimization_barrier(jnp.mean(floats * floats, axis=-1, keepdims=True)) + EPSILON)
    return (floats * factor * norm_gain).astype(jnp.bfloat16)

def block_terms(select_block, decay_block):
    extent = decay_block.shape[1]
    half_width = select_block.shape[1] // 2
    summed = jnp.cumsum(decay_block, axis=1)
    inward = jnp.sqrt(-jnp.expm1(2.0 * decay_block))
    target = lax.broadcasted_iota(jnp.int32, (extent, extent), 0)
    source = lax.broadcasted_iota(jnp.int32, (extent, extent), 1)
    causal = (target >= source).astype(jnp.float32)
    gap_sums = jnp.minimum(summed[:, :, None] - summed[:, None, :], 0.0)
    affinity = jnp.dot(select_block[:, half_width:], select_block[:, :half_width].T, preferred_element_type=jnp.float32)
    mixing = rounded(jnp.exp(gap_sums) * causal * affinity[None] * inward[:, None, :])
    opening = jnp.exp(summed)
    ending = jnp.exp(summed[:, -1:] - summed) * inward
    return (mixing, opening, ending, jnp.exp(summed[:, -1]))

def forward_block(memory, block_piece, skip_gain):
    values, select_block, decay_block = block_piece
    half_width = select_block.shape[1] // 2
    mixing, opening, ending, through = block_terms(select_block, decay_block)
    floats = values.astype(jnp.float32)
    readout = select_block[:, half_width:].astype(jnp.float32)
    writein = select_block[:, :half_width].astype(jnp.float32)
    within = jnp.einsum('hts,shp->thp', mixing, floats, precision=PRECISE)
    carried = jnp.einsum('tn,hpn->thp', readout, memory, precision=PRECISE) * opening.T[:, :, None]
    output = within + carried + skip_gain[None, :, None] * floats
    weighted = rounded(floats * ending.T[:, :, None])
    memory = through[:, None, None] * memory + jnp.einsum('shp,sn->hpn', weighted, writein, precision=PRECISE)
    return (memory, output)

def backward_block(memory, block_piece, skip_gain):
    values, select_block, decay_block = block_piece
    half_width = select_block.shape[1] // 2
    mixing, opening, ending, through = block_terms(select_block, decay_block)
    floats = values.astype(jnp.float32)
    readout = select_block[:, half_width:].astype(jnp.float32)
    writein = select_block[:, :half_width].astype(jnp.float32)
    within = jnp.einsum('hts,thp->shp', mixing, floats, precision=PRECISE)
    carried = jnp.einsum('sn,hpn->shp', writein, memory, precision=PRECISE) * ending.T[:, :, None]
    output = within + carried + skip_gain[None, :, None] * floats
    weighted = rounded(floats * opening.T[:, :, None])
    memory = through[:, None, None] * memory + jnp.einsum('thp,tn->hpn', weighted, readout, precision=PRECISE)
    return (memory, output)

def run_chain(values, select, decay, skip_gain, backward):
    series_extent, model_width = values.shape
    head_count = decay.shape[0]
    half_width = select.shape[1] // 2
    block_size = min(512, TOK_DEV)
    block_count = series_extent // block_size
    pieces = (values.reshape(block_count, block_size, head_count, model_width // head_count), select.reshape(block_count, block_size, select.shape[1]), decay.reshape(head_count, block_count, block_size).transpose(1, 0, 2))
    zero_state = jnp.zeros((head_count, model_width // head_count, half_width), jnp.float32)

    def advance(memory, block_piece):
        if backward:
            return backward_block(memory, block_piece, skip_gain)
        return forward_block(memory, block_piece, skip_gain)
    last_state, results = lax.scan(advance, zero_state, pieces, reverse=backward)
    return results.reshape(series_extent, model_width).astype(jnp.bfloat16)

def mixer_forward(inputs, select, decay, norm_gain, skip_gain, weight_in, weight_out):
    normed = norm_rows(inputs, norm_gain)
    projected = jnp.dot(normed, weight_in, preferred_element_type=jnp.float32).astype(jnp.bfloat16)
    scanned = run_chain(projected, select, decay, skip_gain, False)
    total = inputs.astype(jnp.float32) + jnp.dot(scanned, weight_out, preferred_element_type=jnp.float32)
    return total.astype(jnp.bfloat16)

def mixer_backward(inputs, incoming, select, decay, norm_gain, skip_gain, weight_in, weight_out):
    pulled = jnp.dot(incoming, weight_out.T, preferred_element_type=jnp.float32).astype(jnp.bfloat16)
    scanned = run_chain(pulled, select, decay, skip_gain, True)
    returned = jnp.dot(scanned, weight_in.T, preferred_element_type=jnp.float32)
    floats = inputs.astype(jnp.float32)
    factor = lax.rsqrt(lax.optimization_barrier(jnp.mean(floats * floats, axis=-1, keepdims=True)) + EPSILON)
    scaled = norm_gain * returned
    result = incoming.astype(jnp.float32) + factor * scaled - floats * factor ** 3 * lax.optimization_barrier(jnp.mean(scaled * floats, axis=-1, keepdims=True))
    return result.astype(jnp.bfloat16)

def reference(tokens, row_select, row_decay, row_gain, row_skip, row_in, row_out, col_select, col_decay, col_gain, col_skip, col_in, col_out, cotangent):
    frame_count, row_count, col_count, model_width = tokens.shape
    head_count = row_skip.shape[0]
    doubled = row_select.shape[-1]
    row_inputs = tokens.reshape(-1, model_width)
    row_lam = row_decay.transpose(1, 0, 2, 3).reshape(head_count, -1)
    col_lam = col_decay.transpose(1, 0, 2, 3).reshape(head_count, -1)
    row_mixed = mixer_forward(row_inputs, row_select.reshape(-1, doubled), row_lam, row_gain, row_skip, row_in, row_out)
    col_tokens = row_mixed.reshape(frame_count, row_count, col_count, model_width).transpose(0, 2, 1, 3).reshape(-1, model_width)
    mixed = mixer_forward(col_tokens, col_select.reshape(-1, doubled), col_lam, col_gain, col_skip, col_in, col_out)
    col_grad = mixer_backward(col_tokens, cotangent.reshape(-1, model_width), col_select.reshape(-1, doubled), col_lam, col_gain, col_skip, col_in, col_out)
    row_grad = col_grad.reshape(frame_count, col_count, row_count, model_width).transpose(0, 2, 1, 3).reshape(-1, model_width)
    grad_tokens = mixer_backward(row_inputs, row_grad, row_select.reshape(-1, doubled), row_lam, row_gain, row_skip, row_in, row_out)
    return (mixed.reshape(frame_count, col_count, row_count, model_width), grad_tokens.reshape(frame_count, row_count, col_count, model_width))
```

```python
import functools

import jax
import jax.numpy as jnp
import numpy as np
from jax import lax
from jax.experimental import pallas as pl
from jax.experimental.pallas import tpu as pltpu
from jax.sharding import PartitionSpec as P

EPSILON = 1e-05
F32, BF16 = jnp.float32, jnp.bfloat16
HIGH = lax.Precision.HIGHEST
LANES = 128
PACK = 16


def mm(a, b, ca=1, cb=0, precision=None):
    return lax.dot_general(
        a, b, (((ca,), (cb,)), ((), ())), preferred_element_type=F32, precision=precision
    )


def one_minus_exp(y):
    near = jnp.maximum(y, -0.5)
    series = 1.0 + near * (1.0 / 9.0)
    for k in range(8, 1, -1):
        series = 1.0 + near * (1.0 / k) * series
    return jnp.where(y > -0.5, -near * series, 1.0 - jnp.exp(y))


def constants(T, heads, width, row_share, col_share, peers):
    rows, cols = peers * row_share, peers * col_share
    model = heads * width
    t = np.arange(T)
    tri = (t[:, None] >= t[None, :]).astype(np.float32)
    eye = np.eye(T, dtype=np.float32)
    lane = np.arange(model)
    expand = (lane[None, :] // width == np.arange(heads)[:, None]).astype(np.float32)
    s = np.arange(width)
    diag = (lane[None, :] % width == s[:, None]).astype(np.float32)
    quad = min(4, heads)
    q = np.arange(quad * width) // width
    block = (q[:, None] == q[None, :]).astype(np.float32)
    share = row_share * col_share
    parts = max(1, PACK // share)
    o = np.arange(peers * parts * share)
    d, j, c, r = o // (parts * share), o // share % parts, o // row_share % col_share, o % row_share
    row_from = j * T + r * cols + d * col_share + c
    col_from = j * T + c * rows + d * row_share + r
    i = np.arange(parts * T)
    pack_row = (row_from[:, None] == i[None, :]).astype(np.float32)
    pack_col = (col_from[:, None] == i[None, :]).astype(np.float32)
    as16 = lambda a: jnp.asarray(a.astype(np.float32), BF16)
    return (
        jnp.asarray(tri),
        jnp.asarray(eye),
        jnp.asarray(expand),
        jnp.asarray(diag),
        as16(block),
        as16(pack_row),
        as16(pack_col),
        as16(pack_row.T),
        as16(pack_col.T),
    ), parts


def kernel(
    sizes,
    tokens,
    row_select,
    row_decay,
    row_gain,
    row_skip,
    row_in,
    row_out,
    col_select,
    col_decay,
    col_gain,
    col_skip,
    col_in,
    col_out,
    cotangent,
    tri,
    eye,
    expand,
    diag,
    block,
    pack_row,
    pack_col,
    open_row,
    open_col,
    mixed,
    grad_tokens,
    cum_ref,
    inw_ref,
    scan_ref,
    dec_out,
    dec_in,
    state_out,
    state_in,
    inner,
    frame_in,
    enter_out,
    enter_in,
    swap_out,
    swap_in,
    send_sem,
    recv_sem,
):
    peers, frames, heads, width, parts = sizes
    T, model = tokens.shape
    half = row_select.shape[1] // 2
    blocks = T // width
    me, frame = lax.axis_index("seq"), lax.axis_index("frame")
    strips, halves = model // LANES, half // PACK
    tiles = 2 * strips * halves

    barrier = pltpu.get_barrier_semaphore()

    def greet(o, axis, here, count):
        there = lax.rem(here + o, count)
        pl.semaphore_signal(
            barrier, inc=1, device_id={axis: there}, device_id_type=pl.DeviceIdType.MESH
        )

    lax.fori_loop(1, peers, lambda o, _: (greet(o, "seq", me, peers), 0)[1], 0)
    lax.fori_loop(1, frames, lambda o, _: (greet(o, "frame", frame, frames), 0)[1], 0)

    def remote(src, dst, at, axis, there):
        return pltpu.make_async_remote_copy(
            src_ref=src,
            dst_ref=dst,
            send_sem=send_sem.at[at],
            recv_sem=recv_sem.at[at],
            device_id={axis: there},
            device_id_type=pl.DeviceIdType.MESH,
        )

    def to_peers(src_of, dst, at, owners):
        def one(o, _):
            there = lax.rem(me + o, peers)
            copy = remote(src_of(there), dst.at[me], at, "seq", there)
            if owners and tiles < peers:
                pl.when(there < tiles)(copy.start)
            else:
                copy.start()
            return 0

        lax.fori_loop(1, peers, one, 0)

    def only_owner(do):
        if tiles < peers:
            pl.when(me < tiles)(do)
        else:
            do()

    def arrived(ref, at, count):
        part = ref.at[pl.ds(0, count)]
        pltpu.make_async_copy(part, part, recv_sem.at[at]).wait()

    def sent(ref, at, count):
        def one(_, c):
            pltpu.make_async_copy(ref.at[0], ref.at[0], send_sem.at[at]).wait()
            return c

        lax.fori_loop(0, count, one, 0)

    def decays(m, decay):
        cols = decay.shape[2]
        cum = jnp.zeros((T, heads), F32)
        lam = jnp.zeros((T, heads), F32)
        for r in range(decay.shape[1]):
            piece = decay[:, r, :]
            cum += mm(tri[:, r * cols : (r + 1) * cols], piece, 1, 1, HIGH)
            lam += mm(eye[:, r * cols : (r + 1) * cols], piece, 1, 1, HIGH)
        inward = jnp.sqrt(one_minus_exp(2.0 * lam))
        cum_ref[m] = mm(cum, expand[...], 1, 0, HIGH)
        inw_ref[m] = mm(inward, expand[...], 1, 0, HIGH)

    decays(0, row_decay)
    decays(1, col_decay)
    for m in range(2):
        for j in range(strips):
            dec_out[j, m : m + 1, :] = cum_ref[m, T - 1 : T, j * LANES : (j + 1) * LANES]

    pl.semaphore_wait(barrier, peers - 1 + frames - 1)
    to_peers(lambda there: dec_out.at[lax.rem(there, strips)], dec_in, 0, True)
    dec_in[me] = dec_out[lax.rem(me, strips)]

    def vectors(select):
        both = select[...].astype(F32)
        return both[:, :half].astype(BF16), both[:, half:].astype(BF16)

    picks = (vectors(row_select), vectors(col_select))

    def skip_of(ref):
        return mm(ref[...], expand[...], 1, 0, HIGH)

    skips = (skip_of(row_skip), skip_of(col_skip))

    def decay_to_end(m):
        return jnp.exp(cum_ref[m, T - 1 : T, :] - cum_ref[m]) * inw_ref[m]

    def leaves(m, values, backward):
        factor = jnp.exp(cum_ref[m]) if backward else decay_to_end(m)
        weighted = (values.astype(F32) * factor).astype(BF16)
        return mm(picks[m][1] if backward else picks[m][0], weighted, 0, 0)

    def block_scan(m, slot, b, values, memory, backward):
        at = slice(0, T) if blocks == 1 else pl.ds(pl.multiple_of(b * width, width), width)
        cum, inw = cum_ref[m, at, :], inw_ref[m, at, :]
        spread = jnp.sum(cum * diag[...], axis=0, keepdims=True)
        if blocks == 1:
            b_vec, c_vec = picks[m]
            mine = values
        else:
            both = (col_select if m else row_select)[at, :].astype(F32)
            b_vec, c_vec = both[:, :half].astype(BF16), both[:, half:].astype(BF16)
            mine = scan_ref[slot, at, :].astype(BF16)
        position = lax.broadcasted_iota(jnp.int32, (width, model), 0)
        lane = lax.broadcasted_iota(jnp.int32, (width, model), 1) & (width - 1)
        many = lambda v: jnp.concatenate([v] * heads, axis=0)
        if backward:
            gap, kept = spread - cum, lane >= position
            affinity = mm(b_vec, many(c_vec), 1, 1)
            inward = inw
        else:
            gap, kept = cum - spread, lane <= position
            affinity = mm(c_vec, many(b_vec), 1, 1)
            inward = jnp.sum(inw * diag[...], axis=0, keepdims=True)
        decayed = jnp.exp(jnp.minimum(gap, 0.0)) * affinity * inward
        mixing = jnp.where(kept, decayed, 0.0).astype(BF16)
        wide = block.shape[0]
        pieces = []
        for q in range(model // wide):
            v = mine[:, q * wide : (q + 1) * wide]
            stacked = jnp.concatenate([v] * (wide // width), axis=0) * block[...]
            pieces.append(mm(mixing[:, q * wide : (q + 1) * wide], stacked))
        result = jnp.concatenate(pieces, axis=1) + skips[m] * mine.astype(F32)
        if blocks == 1:
            scan_ref[slot] = result
            return memory
        last = cum[width - 1 : width, :]
        before = jnp.sum(jnp.where(position == 0, cum - lam_of(m, b), 0.0), axis=0, keepdims=True)
        opening, ending = jnp.exp(cum - before), jnp.exp(last - cum) * inw
        read, write = (b_vec, c_vec) if backward else (c_vec, b_vec)
        outer, inner_factor = (ending, opening) if backward else (opening, ending)
        result += mm(read.astype(F32), memory, 1, 0, HIGH) * outer
        scan_ref[slot, at, :] = result
        weighted = (mine.astype(F32) * inner_factor).astype(BF16)
        return jnp.exp(last - before) * memory + mm(write, weighted, 0, 0)

    def lam_of(m, b):
        at = pl.multiple_of(b * width, width)
        here = cum_ref[m, pl.ds(at, width), :][0:1, :]
        prior_at = pl.multiple_of(jnp.maximum(b - 1, 0) * width, width)
        prior = cum_ref[m, pl.ds(prior_at, width), :][width - 1 : width, :]
        return here - jnp.where(b > 0, prior, 0.0)

    def local_scan(m, slot, values, backward):
        zero = jnp.zeros((half, model), F32)
        if blocks == 1:
            block_scan(m, slot, 0, values, zero, backward)
            return
        scan_ref[slot] = values.astype(F32)
        lax.fori_loop(
            0,
            blocks,
            lambda i, memory: block_scan(
                m, slot, (blocks - 1 - i) if backward else i, None, memory, backward
            ),
            zero,
        )

    def stage(e, a, state):
        for i in range(halves):
            for j in range(strips):
                state_out[e, (a * halves + i) * strips + j] = state[
                    i * PACK : (i + 1) * PACK, j * LANES : (j + 1) * LANES
                ].astype(BF16)

    def send_states(e):
        to_peers(lambda there: state_out.at[e, there], state_in.at[e], 1 + 4 * e, True)

        def keep():
            state_in[e, me] = state_out[e, me]

        only_owner(keep)

    def own(e):
        at = 1 + 4 * e
        back = me >= tiles // 2
        if e == 0:
            arrived(dec_in, 0, peers - 1)
        arrived(state_in.at[e], at, peers - 1)
        second = back if e == 0 else jnp.logical_not(back)
        memory = jnp.zeros((PACK, LANES), F32)
        total = jnp.zeros((1, LANES), F32)
        totals = []
        for i in range(peers):
            p = jnp.where(back, peers - 1 - i, i)
            pair = dec_in[p]
            spent = jnp.where(second, pair[1:2, :], pair[0:1, :])
            inner[i] = memory
            totals.append(total)
            memory = jnp.exp(spent) * memory + state_in[e, p].astype(F32)
            total = total + spent
        frame_in[e, frame, 0:PACK, :] = memory
        frame_in[e, frame, PACK : PACK + 8, :] = jnp.broadcast_to(total, (8, LANES))

        def one(o, _):
            there = lax.rem(frame + o, frames)
            remote(frame_in.at[e, frame], frame_in.at[e, frame], at + 1, "frame", there).start()
            return 0

        lax.fori_loop(1, frames, one, 0)
        arrived(frame_in.at[e], at + 1, frames - 1)
        carry = jnp.zeros((PACK, LANES), F32)
        for i in range(frames - 1):
            g = jnp.where(back, frames - 1 - i, i)
            reached = jnp.where(back, g > frame, g < frame)
            new = jnp.exp(frame_in[e, g, PACK : PACK + 1, :]) * carry + frame_in[e, g, 0:PACK, :]
            carry = jnp.where(reached, new, carry)
        for i in range(peers):
            p = jnp.where(back, peers - 1 - i, i)
            enter_out[e, p] = (inner[i] + jnp.exp(totals[i]) * carry).astype(BF16)
        to_peers(lambda there: enter_out.at[e, there], enter_in.at[e], at + 2, False)
        enter_in[e, me] = enter_out[e, me]

    def entering(e):
        if tiles < peers:
            pl.when(me < tiles)(lambda: arrived(enter_in.at[e], 3 + 4 * e, tiles - 1))
            pl.when(me >= tiles)(lambda: arrived(enter_in.at[e], 3 + 4 * e, tiles))
        else:
            arrived(enter_in.at[e], 3 + 4 * e, tiles - 1)
        return tuple(
            jnp.concatenate(
                [
                    jnp.concatenate(
                        [enter_in[e, (a * halves + i) * strips + j] for j in range(strips)], axis=1
                    )
                    for i in range(halves)
                ],
                axis=0,
            )
            for a in range(2)
        )

    def finish_scan(m, slot, state, backward):
        if backward:
            carried = mm(picks[m][0], state) * decay_to_end(m)
        else:
            carried = mm(picks[m][1], state) * jnp.exp(cum_ref[m])
        return (scan_ref[slot] + carried).astype(BF16)

    def factor_of(floats):
        return lax.rsqrt(jnp.mean(floats * floats, axis=-1, keepdims=True) + EPSILON)

    def project(values, gain, weight):
        floats = values.astype(F32)
        normed = (floats * factor_of(floats) * gain[...]).astype(BF16)
        return mm(normed, weight[...]).astype(BF16)

    def input_gradient(values, incoming, scanned, gain, weight):
        returned = mm(scanned, weight[...], 1, 1)
        floats = values.astype(F32)
        factor = factor_of(floats)
        scaled = gain[...] * returned
        inner_mean = jnp.mean(scaled * floats, axis=-1, keepdims=True)
        result = incoming.astype(F32) + factor * scaled - floats * (factor**3 * inner_mean)
        return result.astype(BF16)

    strip = model // parts
    share = T // peers * parts

    def swap_send(e, values, pack):
        stacked = jnp.concatenate(
            [values[:, j * strip : (j + 1) * strip] for j in range(parts)], axis=0
        )
        packed = mm(pack[...], stacked).astype(BF16)
        swap_out[e] = packed.reshape(peers, share, strip)
        to_peers(lambda there: swap_out.at[e, there], swap_in.at[e], 9 + e, False)
        swap_in[e, me] = swap_out[e, me]

    def swap_take(e, pack):
        arrived(swap_in.at[e], 9 + e, peers - 1)
        packed = swap_in[e].reshape(peers * share, strip)
        stacked = mm(pack[...], packed).astype(BF16)
        return jnp.concatenate([stacked[j * T : (j + 1) * T, :] for j in range(parts)], axis=1)

    def ends(m, slot, values, backward):
        return leaves(m, values, backward)

    row_values = project(tokens[...], row_gain, row_in)
    stage(0, 0, ends(0, 0, row_values, False))
    col_pulled = mm(cotangent[...], col_out[...], 1, 1).astype(BF16)
    stage(0, 1, ends(1, 1, col_pulled, True))
    send_states(0)
    local_scan(0, 0, row_values, False)
    local_scan(1, 1, col_pulled, True)
    only_owner(lambda: own(0))
    row_state, col_state = entering(0)
    row_scanned = finish_scan(0, 0, row_state, False)
    row_mixed = (tokens[...].astype(F32) + mm(row_scanned, row_out[...])).astype(BF16)
    swap_send(0, row_mixed, pack_row)
    col_scanned = finish_scan(1, 1, col_state, True)
    col_tokens = swap_take(0, open_col)
    col_grad = input_gradient(col_tokens, cotangent[...], col_scanned, col_gain, col_in)
    swap_send(1, col_grad, pack_col)
    col_values = project(col_tokens, col_gain, col_in)
    stage(1, 0, ends(1, 0, col_values, False))
    local_scan(1, 0, col_values, False)
    row_grad = swap_take(1, open_row)
    row_pulled = mm(row_grad, row_out[...], 1, 1).astype(BF16)
    stage(1, 1, ends(0, 1, row_pulled, True))
    send_states(1)
    local_scan(0, 1, row_pulled, True)
    only_owner(lambda: own(1))
    col_state, row_state = entering(1)
    col_scanned = finish_scan(1, 0, col_state, False)
    mixed[...] = (col_tokens.astype(F32) + mm(col_scanned, col_out[...])).astype(BF16)
    row_scanned = finish_scan(0, 1, row_state, True)
    grad_tokens[...] = input_gradient(tokens[...], row_grad, row_scanned, row_gain, row_in)

    def drain(ref, at, owners):
        if owners and tiles < peers:
            pl.when(me < tiles)(lambda: sent(ref, at, tiles - 1))
            pl.when(me >= tiles)(lambda: sent(ref, at, tiles))
        else:
            sent(ref, at, peers - 1)

    drain(dec_out, 0, True)
    for e in range(2):
        drain(state_out.at[e], 1 + 4 * e, True)
        only_owner(lambda: sent(frame_in.at[e], 2 + 4 * e, frames - 1))
        only_owner(lambda: sent(enter_out.at[e], 3 + 4 * e, peers - 1))
        drain(swap_out.at[e], 9 + e, False)


def body(peers, frames, tokens, row_select, row_decay, row_gain, row_skip, row_in, row_out,
         col_select, col_decay, col_gain, col_skip, col_in, col_out, cotangent):
    model = tokens.shape[-1]
    heads = row_decay.shape[1]
    doubled = row_select.shape[-1]
    half = doubled // 2
    width = model // heads
    flat = tokens.reshape(-1, model)
    T = flat.shape[0]
    fixed, parts = constants(
        T, heads, width, row_decay.shape[2], col_decay.shape[2], peers
    )
    strips = model // LANES
    tiles = 2 * strips * (half // PACK)
    vmem = pl.BlockSpec(memory_space=pltpu.VMEM)
    share = T // peers * parts
    operands = (
        flat,
        row_select.reshape(-1, doubled),
        row_decay.reshape(row_decay.shape[1:]),
        row_gain.reshape(1, -1),
        row_skip.reshape(1, -1),
        row_in,
        row_out,
        col_select.reshape(-1, doubled),
        col_decay.reshape(col_decay.shape[1:]),
        col_gain.reshape(1, -1),
        col_skip.reshape(1, -1),
        col_in,
        col_out,
        cotangent.reshape(-1, model),
    ) + fixed
    out = jax.ShapeDtypeStruct((T, model), BF16)
    mixed, grad = pl.pallas_call(
        functools.partial(kernel, (peers, frames, heads, width, parts)),
        out_shape=(out, out),
        in_specs=[vmem] * len(operands),
        out_specs=(vmem, vmem),
        scratch_shapes=[
            pltpu.VMEM((2, T, model), F32),
            pltpu.VMEM((2, T, model), F32),
            pltpu.VMEM((2, T, model), F32),
            pltpu.VMEM((strips, 2, LANES), F32),
            pltpu.VMEM((peers, 2, LANES), F32),
            pltpu.VMEM((2, tiles, PACK, LANES), BF16),
            pltpu.VMEM((2, peers, PACK, LANES), BF16),
            pltpu.VMEM((peers, PACK, LANES), F32),
            pltpu.VMEM((2, frames, PACK + 8, LANES), F32),
            pltpu.VMEM((2, peers, PACK, LANES), BF16),
            pltpu.VMEM((2, tiles, PACK, LANES), BF16),
            pltpu.VMEM((2, peers, share, model // parts), BF16),
            pltpu.VMEM((2, peers, share, model // parts), BF16),
            pltpu.SemaphoreType.DMA((11,)),
            pltpu.SemaphoreType.DMA((11,)),
        ],
        compiler_params=pltpu.CompilerParams(
            collective_id=0, has_side_effects=True, vmem_limit_bytes=48 * 1024 * 1024
        ),
    )(*operands)
    return (mixed.reshape(cotangent.shape), grad.reshape(tokens.shape))


def solution(mesh):
    token, decay = P("frame", "seq", None, None), P("frame", None, "seq", None)
    mixer = (token, decay, P(), P(), P(), P())
    return jax.shard_map(
        functools.partial(body, mesh.shape["seq"], mesh.shape["frame"]),
        mesh=mesh,
        in_specs=(token,) + mixer + mixer + (token,),
        out_specs=(token, token),
        check_vma=False,
    )
```

```python
import functools

import jax
import jax.numpy as jnp
import numpy as np
from jax import lax
from jax.experimental import pallas as pl
from jax.experimental.pallas import tpu as pltpu
from jax.sharding import PartitionSpec as P

EPSILON = 1e-05
F32, BF16 = jnp.float32, jnp.bfloat16
HIGH = lax.Precision.HIGHEST
LANES = 128
PACK = 16


def mm(a, b, ca=1, cb=0, precision=None):
    return lax.dot_general(
        a, b, (((ca,), (cb,)), ((), ())), preferred_element_type=F32, precision=precision
    )


def one_minus_exp(y):
    near = jnp.maximum(y, -0.5)
    series = 1.0 + near * (1.0 / 9.0)
    for k in range(8, 1, -1):
        series = 1.0 + near * (1.0 / k) * series
    return jnp.where(y > -0.5, -near * series, 1.0 - jnp.exp(y))


def constants(T, heads, width, row_share, col_share, peers):
    rows, cols = peers * row_share, peers * col_share
    model = heads * width
    t = np.arange(T)
    tri = (t[:, None] >= t[None, :]).astype(np.float32)
    eye = np.eye(T, dtype=np.float32)
    lane = np.arange(model)
    expand = (lane[None, :] // width == np.arange(heads)[:, None]).astype(np.float32)
    s = np.arange(width)
    diag = (lane[None, :] % width == s[:, None]).astype(np.float32)
    quad = min(4, heads)
    q = np.arange(quad * width) // width
    block = (q[:, None] == q[None, :]).astype(np.float32)
    share = row_share * col_share
    parts = max(1, PACK // share)
    o = np.arange(peers * parts * share)
    d, j, c, r = o // (parts * share), o // share % parts, o // row_share % col_share, o % row_share
    row_from = j * T + r * cols + d * col_share + c
    col_from = j * T + c * rows + d * row_share + r
    i = np.arange(parts * T)
    pack_row = (row_from[:, None] == i[None, :]).astype(np.float32)
    pack_col = (col_from[:, None] == i[None, :]).astype(np.float32)
    as16 = lambda a: jnp.asarray(a.astype(np.float32), BF16)
    return (
        jnp.asarray(tri),
        jnp.asarray(eye),
        jnp.asarray(expand),
        jnp.asarray(diag),
        as16(block),
        as16(pack_row),
        as16(pack_col),
        as16(pack_row.T),
        as16(pack_col.T),
    ), parts


ORDER = (
    "row_decay",
    "col_decay",
    "tri",
    "eye",
    "expand",
    "tokens",
    "row_gain",
    "row_in",
    "row_select",
    "col_select",
    "row_skip",
    "col_skip",
    "cotangent",
    "col_out",
    "diag",
    "block",
    "row_out",
    "pack_row",
    "open_col",
    "col_gain",
    "col_in",
    "pack_col",
    "open_row",
)
NAMES = (
    "tokens",
    "row_select",
    "row_decay",
    "row_gain",
    "row_skip",
    "row_in",
    "row_out",
    "col_select",
    "col_decay",
    "col_gain",
    "col_skip",
    "col_in",
    "col_out",
    "cotangent",
    "tri",
    "eye",
    "expand",
    "diag",
    "block",
    "pack_row",
    "pack_col",
    "open_row",
    "open_col",
)


def kernel(sizes, *refs):
    count = len(NAMES)
    far = dict(zip(NAMES, refs[:count]))
    mixed, grad_tokens = refs[count : count + 2]
    near = dict(zip(NAMES, refs[count + 2 : 2 * count + 2]))
    (
        load_sem,
        cum_ref,
        inw_ref,
        scan_ref,
        dec_out,
        dec_in,
        state_out,
        state_in,
        enter_out,
        enter_in,
        swap_out,
        swap_in,
        send_sem,
        recv_sem,
        cross_sem,
    ) = refs[2 * count + 2 :]
    loads = {
        name: pltpu.make_async_copy(far[name], near[name], load_sem.at[i])
        for i, name in enumerate(ORDER)
    }
    for name in ORDER:
        loads[name].start()
    ready = iter(ORDER)

    def until(name):
        for one in ready:
            loads[one].wait()
            if one == name:
                break

    tokens = near["tokens"]
    row_select = near["row_select"]
    row_decay = near["row_decay"]
    row_gain = near["row_gain"]
    row_skip = near["row_skip"]
    row_in = near["row_in"]
    row_out = near["row_out"]
    col_select = near["col_select"]
    col_decay = near["col_decay"]
    col_gain = near["col_gain"]
    col_skip = near["col_skip"]
    col_in = near["col_in"]
    col_out = near["col_out"]
    cotangent = near["cotangent"]
    tri = near["tri"]
    eye = near["eye"]
    expand = near["expand"]
    diag = near["diag"]
    block = near["block"]
    pack_row = near["pack_row"]
    pack_col = near["pack_col"]
    open_row = near["open_row"]
    open_col = near["open_col"]
    peers, frames, heads, width, parts = sizes
    T, model = tokens.shape
    half = row_select.shape[1] // 2
    blocks = T // width
    me, frame = lax.axis_index("seq"), lax.axis_index("frame")
    strips, halves = model // LANES, half // PACK
    tiles = 2 * strips * halves

    barrier = pltpu.get_barrier_semaphore()

    def greet(o, axis, here, count):
        there = lax.rem(here + o, count)
        pl.semaphore_signal(
            barrier, inc=1, device_id={axis: there}, device_id_type=pl.DeviceIdType.MESH
        )

    lax.fori_loop(1, peers, lambda o, _: (greet(o, "seq", me, peers), 0)[1], 0)

    def greet_frame(o, _):
        there = lax.rem(frame + o, frames)

        def one(s, c):
            pl.semaphore_signal(
                barrier,
                inc=1,
                device_id={"seq": s, "frame": there},
                device_id_type=pl.DeviceIdType.MESH,
            )
            return c

        return lax.fori_loop(0, peers, one, 0)

    lax.fori_loop(1, frames, greet_frame, 0)

    def remote(src, dst, at, axis, there):
        return pltpu.make_async_remote_copy(
            src_ref=src,
            dst_ref=dst,
            send_sem=send_sem.at[at],
            recv_sem=recv_sem.at[at],
            device_id={axis: there},
            device_id_type=pl.DeviceIdType.MESH,
        )

    def to_peers(src_of, dst, at, owners):
        def one(o, _):
            there = lax.rem(me + o, peers)
            copy = remote(src_of(there), dst.at[me], at, "seq", there)
            if owners and tiles < peers:
                pl.when(there < tiles)(copy.start)
            else:
                copy.start()
            return 0

        lax.fori_loop(1, peers, one, 0)

    def to_frames(src_of, dst, at, slot):
        def one(o, _):
            there = lax.rem(frame + o, frames)
            base = jnp.where(there > frame, 0, tiles // 2)

            def owner(i, c):
                k = base + lax.rem(me + i, tiles // 2)
                pltpu.make_async_remote_copy(
                    src_ref=src_of(k),
                    dst_ref=dst.at[frame, me],
                    send_sem=send_sem.at[at],
                    recv_sem=cross_sem.at[slot, frame],
                    device_id={"seq": k, "frame": there},
                    device_id_type=pl.DeviceIdType.MESH,
                ).start()
                return c

            lax.fori_loop(0, tiles // 2, owner, 0)
            return 0

        lax.fori_loop(1, frames, one, 0)

    def only_owner(do):
        if tiles < peers:
            pl.when(me < tiles)(do)
        else:
            do()

    def arrived(ref, at, count):
        part = ref.at[pl.ds(0, count)]
        pltpu.make_async_copy(part, part, recv_sem.at[at]).wait()

    def all_of(ref, sem):
        pltpu.make_async_copy(ref, ref, sem).wait()

    def sent(ref, at, count):
        def one(_, c):
            pltpu.make_async_copy(ref.at[0], ref.at[0], send_sem.at[at]).wait()
            return c

        lax.fori_loop(0, count, one, 0)

    def decays(m, decay):
        cols = decay.shape[2]
        cum = jnp.zeros((T, heads), F32)
        lam = jnp.zeros((T, heads), F32)
        for r in range(decay.shape[1]):
            piece = decay[:, r, :]
            cum += mm(tri[:, r * cols : (r + 1) * cols], piece, 1, 1, HIGH)
            lam += mm(eye[:, r * cols : (r + 1) * cols], piece, 1, 1, HIGH)
        inward = jnp.sqrt(one_minus_exp(2.0 * lam))
        cum_ref[m] = mm(cum, expand[...], 1, 0, HIGH)
        inw_ref[m] = mm(inward, expand[...], 1, 0, HIGH)

    until("expand")
    decays(0, row_decay)
    decays(1, col_decay)
    for m in range(2):
        for j in range(strips):
            dec_out[j, m : m + 1, :] = cum_ref[m, T - 1 : T, j * LANES : (j + 1) * LANES]

    pl.semaphore_wait(barrier, peers * frames - 1)
    strip_of = lambda there: dec_out.at[lax.rem(there, strips)]
    to_peers(strip_of, dec_in.at[frame], 0, True)
    to_frames(strip_of, dec_in, 0, 2)
    dec_in[frame, me] = dec_out[lax.rem(me, strips)]

    until("col_skip")

    def vectors(select):
        both = select[...].astype(F32)
        return both[:, :half].astype(BF16), both[:, half:].astype(BF16)

    picks = (vectors(row_select), vectors(col_select))

    def skip_of(ref):
        return mm(ref[...], expand[...], 1, 0, HIGH)

    skips = (skip_of(row_skip), skip_of(col_skip))

    def decay_to_end(m):
        return jnp.exp(cum_ref[m, T - 1 : T, :] - cum_ref[m]) * inw_ref[m]

    def leaves(m, values, backward):
        factor = jnp.exp(cum_ref[m]) if backward else decay_to_end(m)
        weighted = (values.astype(F32) * factor).astype(BF16)
        return mm(picks[m][1] if backward else picks[m][0], weighted, 0, 0)

    def block_scan(m, slot, b, values, memory, backward):
        at = slice(0, T) if blocks == 1 else pl.ds(pl.multiple_of(b * width, width), width)
        cum, inw = cum_ref[m, at, :], inw_ref[m, at, :]
        spread = jnp.sum(cum * diag[...], axis=0, keepdims=True)
        if blocks == 1:
            b_vec, c_vec = picks[m]
            mine = values
        else:
            both = (col_select if m else row_select)[at, :].astype(F32)
            b_vec, c_vec = both[:, :half].astype(BF16), both[:, half:].astype(BF16)
            mine = scan_ref[slot, at, :].astype(BF16)
        position = lax.broadcasted_iota(jnp.int32, (width, model), 0)
        lane = lax.broadcasted_iota(jnp.int32, (width, model), 1) & (width - 1)
        many = lambda v: jnp.concatenate([v] * heads, axis=0)
        if backward:
            gap, kept = spread - cum, lane >= position
            affinity = mm(b_vec, many(c_vec), 1, 1)
            inward = inw
        else:
            gap, kept = cum - spread, lane <= position
            affinity = mm(c_vec, many(b_vec), 1, 1)
            inward = jnp.sum(inw * diag[...], axis=0, keepdims=True)
        decayed = jnp.exp(jnp.minimum(gap, 0.0)) * affinity * inward
        mixing = jnp.where(kept, decayed, 0.0).astype(BF16)
        wide = block.shape[0]
        pieces = []
        for q in range(model // wide):
            v = mine[:, q * wide : (q + 1) * wide]
            stacked = jnp.concatenate([v] * (wide // width), axis=0) * block[...]
            pieces.append(mm(mixing[:, q * wide : (q + 1) * wide], stacked))
        result = jnp.concatenate(pieces, axis=1) + skips[m] * mine.astype(F32)
        if blocks == 1:
            scan_ref[slot] = result
            return memory
        last = cum[width - 1 : width, :]
        before = jnp.sum(jnp.where(position == 0, cum - lam_of(m, b), 0.0), axis=0, keepdims=True)
        opening, ending = jnp.exp(cum - before), jnp.exp(last - cum) * inw
        read, write = (b_vec, c_vec) if backward else (c_vec, b_vec)
        outer, inner_factor = (ending, opening) if backward else (opening, ending)
        result += mm(read.astype(F32), memory, 1, 0, HIGH) * outer
        scan_ref[slot, at, :] = result
        weighted = (mine.astype(F32) * inner_factor).astype(BF16)
        return jnp.exp(last - before) * memory + mm(write, weighted, 0, 0)

    def lam_of(m, b):
        at = pl.multiple_of(b * width, width)
        here = cum_ref[m, pl.ds(at, width), :][0:1, :]
        prior_at = pl.multiple_of(jnp.maximum(b - 1, 0) * width, width)
        prior = cum_ref[m, pl.ds(prior_at, width), :][width - 1 : width, :]
        return here - jnp.where(b > 0, prior, 0.0)

    def local_scan(m, slot, values, backward):
        zero = jnp.zeros((half, model), F32)
        if blocks == 1:
            block_scan(m, slot, 0, values, zero, backward)
            return
        scan_ref[slot] = values.astype(F32)
        lax.fori_loop(
            0,
            blocks,
            lambda i, memory: block_scan(
                m, slot, (blocks - 1 - i) if backward else i, None, memory, backward
            ),
            zero,
        )

    def stage(e, a, state):
        for i in range(halves):
            for j in range(strips):
                state_out[e, (a * halves + i) * strips + j] = state[
                    i * PACK : (i + 1) * PACK, j * LANES : (j + 1) * LANES
                ].astype(BF16)

    def send_states(e):
        tile_of = lambda there: state_out.at[e, there]
        to_peers(tile_of, state_in.at[e, frame], 1 + 4 * e, True)
        to_frames(tile_of, state_in.at[e], 1 + 4 * e, e)

        def keep():
            state_in[e, frame, me] = state_out[e, me]

        only_owner(keep)

    def own(e):
        at = 1 + 4 * e
        back = me >= tiles // 2
        second = back if e == 0 else jnp.logical_not(back)

        def step(g, i, memory):
            p = jnp.where(back, peers - 1 - i, i)
            pair = dec_in[g, p]
            spent = jnp.where(second, pair[1:2, :], pair[0:1, :])
            return jnp.exp(spent) * memory + state_in[e, g, p].astype(F32)

        def through(o, memory):
            g = jnp.where(back, frames - 1 - o, o)
            if e == 0:
                all_of(dec_in.at[g], cross_sem.at[2, g])
            all_of(state_in.at[e, g], cross_sem.at[e, g])
            for i in range(peers):
                memory = step(g, i, memory)
            return memory

        if e == 0:
            arrived(dec_in.at[frame], 0, peers - 1)
        arrived(state_in.at[e, frame], at, peers - 1)
        memory = lax.fori_loop(
            0,
            jnp.where(back, frames - 1 - frame, frame),
            through,
            jnp.zeros((PACK, LANES), F32),
        )
        for i in range(peers):
            p = jnp.where(back, peers - 1 - i, i)
            enter_out[e, p] = memory.astype(BF16)
            if i < peers - 1:
                memory = step(frame, i, memory)
        to_peers(lambda there: enter_out.at[e, there], enter_in.at[e], at + 2, False)
        enter_in[e, me] = enter_out[e, me]

    def entering(e):
        if tiles < peers:
            pl.when(me < tiles)(lambda: arrived(enter_in.at[e], 3 + 4 * e, tiles - 1))
            pl.when(me >= tiles)(lambda: arrived(enter_in.at[e], 3 + 4 * e, tiles))
        else:
            arrived(enter_in.at[e], 3 + 4 * e, tiles - 1)
        return tuple(
            jnp.concatenate(
                [
                    jnp.concatenate(
                        [enter_in[e, (a * halves + i) * strips + j] for j in range(strips)], axis=1
                    )
                    for i in range(halves)
                ],
                axis=0,
            )
            for a in range(2)
        )

    def finish_scan(m, slot, state, backward):
        if backward:
            carried = mm(picks[m][0], state) * decay_to_end(m)
        else:
            carried = mm(picks[m][1], state) * jnp.exp(cum_ref[m])
        return (scan_ref[slot] + carried).astype(BF16)

    def factor_of(floats):
        return lax.rsqrt(jnp.mean(floats * floats, axis=-1, keepdims=True) + EPSILON)

    def project(values, gain, weight):
        floats = values.astype(F32)
        normed = (floats * factor_of(floats) * gain[...]).astype(BF16)
        return mm(normed, weight[...]).astype(BF16)

    def input_gradient(values, incoming, scanned, gain, weight):
        returned = mm(scanned, weight[...], 1, 1)
        floats = values.astype(F32)
        factor = factor_of(floats)
        scaled = gain[...] * returned
        inner_mean = jnp.mean(scaled * floats, axis=-1, keepdims=True)
        result = incoming.astype(F32) + factor * scaled - floats * (factor**3 * inner_mean)
        return result.astype(BF16)

    strip = model // parts
    share = T // peers * parts

    def swap_send(e, values, pack):
        stacked = jnp.concatenate(
            [values[:, j * strip : (j + 1) * strip] for j in range(parts)], axis=0
        )
        packed = mm(pack[...], stacked).astype(BF16)
        swap_out[e] = packed.reshape(peers, share, strip)
        to_peers(lambda there: swap_out.at[e, there], swap_in.at[e], 9 + e, False)
        swap_in[e, me] = swap_out[e, me]

    def swap_take(e, pack):
        arrived(swap_in.at[e], 9 + e, peers - 1)
        packed = swap_in[e].reshape(peers * share, strip)
        stacked = mm(pack[...], packed).astype(BF16)
        return jnp.concatenate([stacked[j * T : (j + 1) * T, :] for j in range(parts)], axis=1)

    def ends(m, slot, values, backward):
        return leaves(m, values, backward)

    row_values = project(tokens[...], row_gain, row_in)
    stage(0, 0, ends(0, 0, row_values, False))
    until("col_out")
    col_pulled = mm(cotangent[...], col_out[...], 1, 1).astype(BF16)
    stage(0, 1, ends(1, 1, col_pulled, True))
    send_states(0)
    until("block")
    local_scan(0, 0, row_values, False)
    local_scan(1, 1, col_pulled, True)
    until("open_row")
    only_owner(lambda: own(0))
    row_state, col_state = entering(0)
    row_scanned = finish_scan(0, 0, row_state, False)
    row_mixed = (tokens[...].astype(F32) + mm(row_scanned, row_out[...])).astype(BF16)
    swap_send(0, row_mixed, pack_row)
    col_scanned = finish_scan(1, 1, col_state, True)
    col_tokens = swap_take(0, open_col)
    col_grad = input_gradient(col_tokens, cotangent[...], col_scanned, col_gain, col_in)
    swap_send(1, col_grad, pack_col)
    col_values = project(col_tokens, col_gain, col_in)
    stage(1, 0, ends(1, 0, col_values, False))
    local_scan(1, 0, col_values, False)
    row_grad = swap_take(1, open_row)
    row_pulled = mm(row_grad, row_out[...], 1, 1).astype(BF16)
    stage(1, 1, ends(0, 1, row_pulled, True))
    send_states(1)
    local_scan(0, 1, row_pulled, True)
    only_owner(lambda: own(1))
    col_state, row_state = entering(1)
    col_scanned = finish_scan(1, 0, col_state, False)
    mixed[...] = (col_tokens.astype(F32) + mm(col_scanned, col_out[...])).astype(BF16)
    row_scanned = finish_scan(0, 1, row_state, True)
    grad_tokens[...] = input_gradient(tokens[...], row_grad, row_scanned, row_gain, row_in)

    def drain(ref, at, owners):
        if owners and tiles < peers:
            pl.when(me < tiles)(lambda: sent(ref, at, tiles - 1))
            pl.when(me >= tiles)(lambda: sent(ref, at, tiles))
        else:
            sent(ref, at, peers - 1)

    drain(dec_out, 0, True)
    sent(dec_out, 0, (frames - 1) * (tiles // 2))
    for e in range(2):
        drain(state_out.at[e], 1 + 4 * e, True)
        sent(state_out.at[e], 1 + 4 * e, (frames - 1) * (tiles // 2))
        only_owner(lambda: sent(enter_out.at[e], 3 + 4 * e, peers - 1))
        drain(swap_out.at[e], 9 + e, False)


def body(peers, frames, tokens, row_select, row_decay, row_gain, row_skip, row_in, row_out,
         col_select, col_decay, col_gain, col_skip, col_in, col_out, cotangent):
    model = tokens.shape[-1]
    heads = row_decay.shape[1]
    doubled = row_select.shape[-1]
    half = doubled // 2
    width = model // heads
    flat = tokens.reshape(-1, model)
    T = flat.shape[0]
    fixed, parts = constants(
        T, heads, width, row_decay.shape[2], col_decay.shape[2], peers
    )
    strips = model // LANES
    tiles = 2 * strips * (half // PACK)
    vmem = pl.BlockSpec(memory_space=pltpu.VMEM)
    share = T // peers * parts
    operands = (
        flat,
        row_select.reshape(-1, doubled),
        row_decay.reshape(row_decay.shape[1:]),
        row_gain.reshape(1, -1),
        row_skip.reshape(1, -1),
        row_in,
        row_out,
        col_select.reshape(-1, doubled),
        col_decay.reshape(col_decay.shape[1:]),
        col_gain.reshape(1, -1),
        col_skip.reshape(1, -1),
        col_in,
        col_out,
        cotangent.reshape(-1, model),
    ) + fixed
    out = jax.ShapeDtypeStruct((T, model), BF16)
    mixed, grad = pl.pallas_call(
        functools.partial(kernel, (peers, frames, heads, width, parts)),
        out_shape=(out, out),
        in_specs=[pl.BlockSpec(memory_space=pltpu.HBM)] * len(operands),
        out_specs=(vmem, vmem),
        scratch_shapes=[pltpu.VMEM(a.shape, a.dtype) for a in operands]
        + [
            pltpu.SemaphoreType.DMA((len(operands),)),
            pltpu.VMEM((2, T, model), F32),
            pltpu.VMEM((2, T, model), F32),
            pltpu.VMEM((2, T, model), F32),
            pltpu.VMEM((strips, 2, LANES), F32),
            pltpu.VMEM((frames, peers, 2, LANES), F32),
            pltpu.VMEM((2, tiles, PACK, LANES), BF16),
            pltpu.VMEM((2, frames, peers, PACK, LANES), BF16),
            pltpu.VMEM((2, peers, PACK, LANES), BF16),
            pltpu.VMEM((2, tiles, PACK, LANES), BF16),
            pltpu.VMEM((2, peers, share, model // parts), BF16),
            pltpu.VMEM((2, peers, share, model // parts), BF16),
            pltpu.SemaphoreType.DMA((11,)),
            pltpu.SemaphoreType.DMA((11,)),
            pltpu.SemaphoreType.DMA((3, frames)),
        ],
        compiler_params=pltpu.CompilerParams(
            collective_id=0, has_side_effects=True, vmem_limit_bytes=62 * 1024 * 1024
        ),
    )(*operands)
    return (mixed.reshape(cotangent.shape), grad.reshape(tokens.shape))


def solution(mesh):
    token, decay = P("frame", "seq", None, None), P("frame", None, "seq", None)
    mixer = (token, decay, P(), P(), P(), P())
    return jax.shard_map(
        functools.partial(body, mesh.shape["seq"], mesh.shape["frame"]),
        mesh=mesh,
        in_specs=(token,) + mixer + mixer + (token,),
        out_specs=(token, token),
        check_vma=False,
    )
```

```python
import functools

import jax
import jax.numpy as jnp
import numpy as np
from jax import lax
from jax.experimental import pallas as pl
from jax.experimental.pallas import tpu as pltpu
from jax.sharding import PartitionSpec as P

EPSILON = 1e-05
F32, BF16 = jnp.float32, jnp.bfloat16
HIGH = lax.Precision.HIGHEST
LANES = 128
PACK = 16


def mm(a, b, ca=1, cb=0, precision=None):
    return lax.dot_general(
        a, b, (((ca,), (cb,)), ((), ())), preferred_element_type=F32, precision=precision
    )


def one_minus_exp(y):
    near = jnp.maximum(y, -0.5)
    series = 1.0 + near * (1.0 / 9.0)
    for k in range(8, 1, -1):
        series = 1.0 + near * (1.0 / k) * series
    return jnp.where(y > -0.5, -near * series, 1.0 - jnp.exp(y))


def constants(T, heads, width, row_share, col_share, peers):
    rows, cols = peers * row_share, peers * col_share
    model = heads * width
    t = np.arange(T)
    tri = (t[:, None] >= t[None, :]).astype(np.float32)
    eye = np.eye(T, dtype=np.float32)
    lane = np.arange(model)
    expand = (lane[None, :] // width == np.arange(heads)[:, None]).astype(np.float32)
    s = np.arange(width)
    diag = (lane[None, :] % width == s[:, None]).astype(np.float32)
    quad = min(4, heads)
    q = np.arange(quad * width) // width
    block = (q[:, None] == q[None, :]).astype(np.float32)
    share = row_share * col_share
    parts = max(1, PACK // share)
    o = np.arange(peers * parts * share)
    d, j, c, r = o // (parts * share), o // share % parts, o // row_share % col_share, o % row_share
    row_from = j * T + r * cols + d * col_share + c
    col_from = j * T + c * rows + d * row_share + r
    i = np.arange(parts * T)
    pack_row = (row_from[:, None] == i[None, :]).astype(np.float32)
    pack_col = (col_from[:, None] == i[None, :]).astype(np.float32)
    as16 = lambda a: jnp.asarray(a.astype(np.float32), BF16)
    return (
        jnp.asarray(tri),
        jnp.asarray(eye),
        jnp.asarray(expand),
        jnp.asarray(diag),
        as16(block),
        as16(pack_row),
        as16(pack_col),
        as16(pack_row.T),
        as16(pack_col.T),
    ), parts


ORDER = (
    "row_decay",
    "col_decay",
    "tri",
    "eye",
    "expand",
    "tokens",
    "row_gain",
    "row_in",
    "row_select",
    "col_select",
    "row_skip",
    "col_skip",
    "cotangent",
    "col_out",
    "diag",
    "block",
    "row_out",
    "pack_row",
    "open_col",
    "col_gain",
    "col_in",
    "pack_col",
    "open_row",
)
NAMES = (
    "tokens",
    "row_select",
    "row_decay",
    "row_gain",
    "row_skip",
    "row_in",
    "row_out",
    "col_select",
    "col_decay",
    "col_gain",
    "col_skip",
    "col_in",
    "col_out",
    "cotangent",
    "tri",
    "eye",
    "expand",
    "diag",
    "block",
    "pack_row",
    "pack_col",
    "open_row",
    "open_col",
)


def kernel(sizes, *refs):
    count = len(NAMES)
    far = dict(zip(NAMES, refs[:count]))
    mixed, grad_tokens = refs[count : count + 2]
    near = dict(zip(NAMES, refs[count + 2 : 2 * count + 2]))
    (
        load_sem,
        cum_ref,
        inw_ref,
        scan_ref,
        dec_out,
        dec_in,
        state_out,
        state_in,
        enter_out,
        enter_in,
        swap_out,
        swap_in,
        send_sem,
        recv_sem,
        cross_sem,
    ) = refs[2 * count + 2 :]
    loads = {
        name: pltpu.make_async_copy(far[name], near[name], load_sem.at[i])
        for i, name in enumerate(ORDER)
    }
    for name in ORDER:
        loads[name].start()
    ready = iter(ORDER)

    def until(name):
        for one in ready:
            loads[one].wait()
            if one == name:
                break

    tokens = near["tokens"]
    row_select = near["row_select"]
    row_decay = near["row_decay"]
    row_gain = near["row_gain"]
    row_skip = near["row_skip"]
    row_in = near["row_in"]
    row_out = near["row_out"]
    col_select = near["col_select"]
    col_decay = near["col_decay"]
    col_gain = near["col_gain"]
    col_skip = near["col_skip"]
    col_in = near["col_in"]
    col_out = near["col_out"]
    cotangent = near["cotangent"]
    tri = near["tri"]
    eye = near["eye"]
    expand = near["expand"]
    diag = near["diag"]
    block = near["block"]
    pack_row = near["pack_row"]
    pack_col = near["pack_col"]
    open_row = near["open_row"]
    open_col = near["open_col"]
    peers, frames, heads, width, parts = sizes
    T, model = tokens.shape
    half = row_select.shape[1] // 2
    blocks = T // width
    me, frame = lax.axis_index("seq"), lax.axis_index("frame")
    strips, halves = model // LANES, half // PACK
    tiles = 2 * strips * halves

    barrier = pltpu.get_barrier_semaphore()

    def greet(o, axis, here, count):
        there = lax.rem(here + o, count)
        pl.semaphore_signal(
            barrier, inc=1, device_id={axis: there}, device_id_type=pl.DeviceIdType.MESH
        )

    lax.fori_loop(1, peers, lambda o, _: (greet(o, "seq", me, peers), 0)[1], 0)

    def greet_frame(o, _):
        there = lax.rem(frame + o, frames)

        def one(s, c):
            pl.semaphore_signal(
                barrier,
                inc=1,
                device_id={"seq": s, "frame": there},
                device_id_type=pl.DeviceIdType.MESH,
            )
            return c

        return lax.fori_loop(0, peers, one, 0)

    lax.fori_loop(1, frames, greet_frame, 0)

    def remote(src, dst, at, axis, there):
        return pltpu.make_async_remote_copy(
            src_ref=src,
            dst_ref=dst,
            send_sem=send_sem.at[at],
            recv_sem=recv_sem.at[at],
            device_id={axis: there},
            device_id_type=pl.DeviceIdType.MESH,
        )

    def to_peers(src_of, dst, at, owners):
        def one(o, _):
            there = lax.rem(me + o, peers)
            copy = remote(src_of(there), dst.at[me], at, "seq", there)
            if owners and tiles < peers:
                pl.when(there < tiles)(copy.start)
            else:
                copy.start()
            return 0

        lax.fori_loop(1, peers, one, 0)

    def to_frames(src_of, dst, at, slot):
        def one(o, _):
            there = lax.rem(frame + o, frames)
            base = jnp.where(there > frame, 0, 1)

            def owner(i, c):
                k = base + 2 * lax.rem(me // 2 + i, tiles // 2)
                pltpu.make_async_remote_copy(
                    src_ref=src_of(k),
                    dst_ref=dst.at[frame, me],
                    send_sem=send_sem.at[at],
                    recv_sem=cross_sem.at[slot, frame],
                    device_id={"seq": k, "frame": there},
                    device_id_type=pl.DeviceIdType.MESH,
                ).start()
                return c

            lax.fori_loop(0, tiles // 2, owner, 0)
            return 0

        lax.fori_loop(1, frames, one, 0)

    def only_owner(do):
        if tiles < peers:
            pl.when(me < tiles)(do)
        else:
            do()

    def arrived(ref, at, count):
        part = ref.at[pl.ds(0, count)]
        pltpu.make_async_copy(part, part, recv_sem.at[at]).wait()

    def all_of(ref, sem):
        pltpu.make_async_copy(ref, ref, sem).wait()

    def sent(ref, at, count):
        def one(_, c):
            pltpu.make_async_copy(ref.at[0], ref.at[0], send_sem.at[at]).wait()
            return c

        lax.fori_loop(0, count, one, 0)

    def decays(m, decay):
        cols = decay.shape[2]
        cum = jnp.zeros((T, heads), F32)
        lam = jnp.zeros((T, heads), F32)
        for r in range(decay.shape[1]):
            piece = decay[:, r, :]
            cum += mm(tri[:, r * cols : (r + 1) * cols], piece, 1, 1, HIGH)
            lam += mm(eye[:, r * cols : (r + 1) * cols], piece, 1, 1, HIGH)
        inward = jnp.sqrt(one_minus_exp(2.0 * lam))
        cum_ref[m] = mm(cum, expand[...], 1, 0, HIGH)
        inw_ref[m] = mm(inward, expand[...], 1, 0, HIGH)

    until("expand")
    decays(0, row_decay)
    decays(1, col_decay)
    for m in range(2):
        for j in range(strips):
            dec_out[j, m : m + 1, :] = cum_ref[m, T - 1 : T, j * LANES : (j + 1) * LANES]

    pl.semaphore_wait(barrier, peers * frames - 1)
    strip_of = lambda there: dec_out.at[lax.rem(there // 2, strips)]
    to_peers(strip_of, dec_in.at[frame], 0, True)
    to_frames(strip_of, dec_in, 0, 2)
    dec_in[frame, me] = dec_out[lax.rem(me // 2, strips)]

    until("col_skip")

    def vectors(select):
        both = select[...].astype(F32)
        return both[:, :half].astype(BF16), both[:, half:].astype(BF16)

    picks = (vectors(row_select), vectors(col_select))

    def skip_of(ref):
        return mm(ref[...], expand[...], 1, 0, HIGH)

    skips = (skip_of(row_skip), skip_of(col_skip))

    def decay_to_end(m):
        return jnp.exp(cum_ref[m, T - 1 : T, :] - cum_ref[m]) * inw_ref[m]

    def leaves(m, values, backward):
        factor = jnp.exp(cum_ref[m]) if backward else decay_to_end(m)
        weighted = (values.astype(F32) * factor).astype(BF16)
        return mm(picks[m][1] if backward else picks[m][0], weighted, 0, 0)

    def block_scan(m, slot, b, values, memory, backward):
        at = slice(0, T) if blocks == 1 else pl.ds(pl.multiple_of(b * width, width), width)
        cum, inw = cum_ref[m, at, :], inw_ref[m, at, :]
        spread = jnp.sum(cum * diag[...], axis=0, keepdims=True)
        if blocks == 1:
            b_vec, c_vec = picks[m]
            mine = values
        else:
            both = (col_select if m else row_select)[at, :].astype(F32)
            b_vec, c_vec = both[:, :half].astype(BF16), both[:, half:].astype(BF16)
            mine = scan_ref[slot, at, :].astype(BF16)
        position = lax.broadcasted_iota(jnp.int32, (width, model), 0)
        lane = lax.broadcasted_iota(jnp.int32, (width, model), 1) & (width - 1)
        many = lambda v: jnp.concatenate([v] * heads, axis=0)
        if backward:
            gap, kept = spread - cum, lane >= position
            affinity = mm(b_vec, many(c_vec), 1, 1)
            inward = inw
        else:
            gap, kept = cum - spread, lane <= position
            affinity = mm(c_vec, many(b_vec), 1, 1)
            inward = jnp.sum(inw * diag[...], axis=0, keepdims=True)
        decayed = jnp.exp(jnp.minimum(gap, 0.0)) * affinity * inward
        mixing = jnp.where(kept, decayed, 0.0).astype(BF16)
        wide = block.shape[0]
        pieces = []
        for q in range(model // wide):
            v = mine[:, q * wide : (q + 1) * wide]
            stacked = jnp.concatenate([v] * (wide // width), axis=0) * block[...]
            pieces.append(mm(mixing[:, q * wide : (q + 1) * wide], stacked))
        result = jnp.concatenate(pieces, axis=1) + skips[m] * mine.astype(F32)
        if blocks == 1:
            scan_ref[slot] = result
            return memory
        last = cum[width - 1 : width, :]
        before = jnp.sum(jnp.where(position == 0, cum - lam_of(m, b), 0.0), axis=0, keepdims=True)
        opening, ending = jnp.exp(cum - before), jnp.exp(last - cum) * inw
        read, write = (b_vec, c_vec) if backward else (c_vec, b_vec)
        outer, inner_factor = (ending, opening) if backward else (opening, ending)
        result += mm(read.astype(F32), memory, 1, 0, HIGH) * outer
        scan_ref[slot, at, :] = result
        weighted = (mine.astype(F32) * inner_factor).astype(BF16)
        return jnp.exp(last - before) * memory + mm(write, weighted, 0, 0)

    def lam_of(m, b):
        at = pl.multiple_of(b * width, width)
        here = cum_ref[m, pl.ds(at, width), :][0:1, :]
        prior_at = pl.multiple_of(jnp.maximum(b - 1, 0) * width, width)
        prior = cum_ref[m, pl.ds(prior_at, width), :][width - 1 : width, :]
        return here - jnp.where(b > 0, prior, 0.0)

    def local_scan(m, slot, values, backward):
        zero = jnp.zeros((half, model), F32)
        if blocks == 1:
            block_scan(m, slot, 0, values, zero, backward)
            return
        scan_ref[slot] = values.astype(F32)
        lax.fori_loop(
            0,
            blocks,
            lambda i, memory: block_scan(
                m, slot, (blocks - 1 - i) if backward else i, None, memory, backward
            ),
            zero,
        )

    def stage(e, a, state):
        for i in range(halves):
            for j in range(strips):
                state_out[e, 2 * (i * strips + j) + a] = state[
                    i * PACK : (i + 1) * PACK, j * LANES : (j + 1) * LANES
                ].astype(BF16)

    def owns(a):
        return jnp.logical_and(lax.rem(me, 2) == a, me < tiles)

    def send_states(e, a):
        count = tiles // 2
        at = 1 + 4 * e

        def one(i, c):
            k = a + 2 * lax.rem(me // 2 + 1 + i, count)
            copy = remote(state_out.at[e, k], state_in.at[e, frame, me], at, "seq", k)
            pl.when(k != me)(copy.start)
            return c

        lax.fori_loop(0, count, one, 0)

        def keep():
            state_in[e, frame, me] = state_out[e, me]

        pl.when(owns(a))(keep)

        def onward(o, _):
            there = frame + 1 + o if a == 0 else frame - 1 - o

            def owner(i, c):
                k = a + 2 * lax.rem(me // 2 + i, count)
                pltpu.make_async_remote_copy(
                    src_ref=state_out.at[e, k],
                    dst_ref=state_in.at[e, frame, me],
                    send_sem=send_sem.at[at],
                    recv_sem=cross_sem.at[e, frame],
                    device_id={"seq": k, "frame": there},
                    device_id_type=pl.DeviceIdType.MESH,
                ).start()
                return c

            return lax.fori_loop(0, count, owner, 0)

        lax.fori_loop(0, frames - 1 - frame if a == 0 else frame, onward, 0)

    def own(e):
        at = 1 + 4 * e
        back = lax.rem(me, 2) == 1
        second = back if e == 0 else jnp.logical_not(back)

        def step(g, i, memory):
            p = jnp.where(back, peers - 1 - i, i)
            pair = dec_in[g, p]
            spent = jnp.where(second, pair[1:2, :], pair[0:1, :])
            return jnp.exp(spent) * memory + state_in[e, g, p].astype(F32)

        def through(o, memory):
            g = jnp.where(back, frames - 1 - o, o)
            if e == 0:
                all_of(dec_in.at[g], cross_sem.at[2, g])
            all_of(state_in.at[e, g], cross_sem.at[e, g])
            for i in range(peers):
                memory = step(g, i, memory)
            return memory

        if e == 0:
            arrived(dec_in.at[frame], 0, peers - 1)
        arrived(state_in.at[e, frame], at, peers - 1)
        memory = lax.fori_loop(
            0,
            jnp.where(back, frames - 1 - frame, frame),
            through,
            jnp.zeros((PACK, LANES), F32),
        )
        for i in range(peers):
            p = jnp.where(back, peers - 1 - i, i)
            enter_out[e, p] = memory.astype(BF16)
            if i < peers - 1:
                memory = step(frame, i, memory)
        landing = at + 1 + jnp.where(back, 1, 0)
        to_peers(lambda there: enter_out.at[e, there], enter_in.at[e], landing, False)
        enter_in[e, me] = enter_out[e, me]

    def entering(e, a):
        count = tiles // 2
        at = 2 + 4 * e + a
        pl.when(owns(a))(lambda: arrived(enter_in.at[e], at, count - 1))
        pl.when(jnp.logical_not(owns(a)))(lambda: arrived(enter_in.at[e], at, count))
        return jnp.concatenate(
            [
                jnp.concatenate(
                    [enter_in[e, 2 * (i * strips + j) + a] for j in range(strips)], axis=1
                )
                for i in range(halves)
            ],
            axis=0,
        )

    def finish_scan(m, slot, state, backward):
        if backward:
            carried = mm(picks[m][0], state) * decay_to_end(m)
        else:
            carried = mm(picks[m][1], state) * jnp.exp(cum_ref[m])
        return (scan_ref[slot] + carried).astype(BF16)

    def factor_of(floats):
        return lax.rsqrt(jnp.mean(floats * floats, axis=-1, keepdims=True) + EPSILON)

    def project(values, gain, weight):
        floats = values.astype(F32)
        normed = (floats * factor_of(floats) * gain[...]).astype(BF16)
        return mm(normed, weight[...]).astype(BF16)

    def input_gradient(values, incoming, returned, gain):
        floats = values.astype(F32)
        factor = factor_of(floats)
        scaled = gain[...] * returned
        inner_mean = jnp.mean(scaled * floats, axis=-1, keepdims=True)
        result = incoming.astype(F32) + factor * scaled - floats * (factor**3 * inner_mean)
        return result.astype(BF16)

    strip = model // parts
    share = T // peers * parts

    def swap_send(e, values, pack):
        stacked = jnp.concatenate(
            [values[:, j * strip : (j + 1) * strip] for j in range(parts)], axis=0
        )
        packed = mm(pack[...], stacked).astype(BF16)
        swap_out[e] = packed.reshape(peers, share, strip)
        to_peers(lambda there: swap_out.at[e, there], swap_in.at[e], 9 + e, False)
        swap_in[e, me] = swap_out[e, me]

    def swap_take(e, pack):
        arrived(swap_in.at[e], 9 + e, peers - 1)
        packed = swap_in[e].reshape(peers * share, strip)
        stacked = mm(pack[...], packed).astype(BF16)
        return jnp.concatenate([stacked[j * T : (j + 1) * T, :] for j in range(parts)], axis=1)

    row_values = project(tokens[...], row_gain, row_in)
    stage(0, 0, leaves(0, row_values, False))
    send_states(0, 0)
    until("col_out")
    col_pulled = mm(cotangent[...], col_out[...], 1, 1).astype(BF16)
    stage(0, 1, leaves(1, col_pulled, True))
    send_states(0, 1)
    until("block")
    local_scan(0, 0, row_values, False)
    local_scan(1, 1, col_pulled, True)
    until("open_row")
    only_owner(lambda: own(0))
    row_scanned = finish_scan(0, 0, entering(0, 0), False)
    row_mixed = (tokens[...].astype(F32) + mm(row_scanned, row_out[...])).astype(BF16)
    swap_send(0, row_mixed, pack_row)
    col_scanned = finish_scan(1, 1, entering(0, 1), True)
    col_returned = mm(col_scanned, col_in[...], 1, 1)
    col_tokens = swap_take(0, open_col)
    col_grad = input_gradient(col_tokens, cotangent[...], col_returned, col_gain)
    swap_send(1, col_grad, pack_col)
    col_values = project(col_tokens, col_gain, col_in)
    stage(1, 0, leaves(1, col_values, False))
    send_states(1, 0)
    local_scan(1, 0, col_values, False)
    row_grad = swap_take(1, open_row)
    row_pulled = mm(row_grad, row_out[...], 1, 1).astype(BF16)
    stage(1, 1, leaves(0, row_pulled, True))
    send_states(1, 1)
    local_scan(0, 1, row_pulled, True)
    only_owner(lambda: own(1))
    col_scanned = finish_scan(1, 0, entering(1, 0), False)
    mixed[...] = (col_tokens.astype(F32) + mm(col_scanned, col_out[...])).astype(BF16)
    row_scanned = finish_scan(0, 1, entering(1, 1), True)
    row_returned = mm(row_scanned, row_in[...], 1, 1)
    grad_tokens[...] = input_gradient(tokens[...], row_grad, row_returned, row_gain)

    def drain(ref, at, owners):
        if owners and tiles < peers:
            pl.when(me < tiles)(lambda: sent(ref, at, tiles - 1))
            pl.when(me >= tiles)(lambda: sent(ref, at, tiles))
        else:
            sent(ref, at, peers - 1)

    drain(dec_out, 0, True)
    sent(dec_out, 0, (frames - 1) * (tiles // 2))
    for e in range(2):
        drain(state_out.at[e], 1 + 4 * e, True)
        sent(state_out.at[e], 1 + 4 * e, (frames - 1) * (tiles // 2))
        landing = 2 + 4 * e + lax.rem(me, 2)
        only_owner(lambda: sent(enter_out.at[e], landing, peers - 1))
        drain(swap_out.at[e], 9 + e, False)


def body(peers, frames, tokens, row_select, row_decay, row_gain, row_skip, row_in, row_out,
         col_select, col_decay, col_gain, col_skip, col_in, col_out, cotangent):
    model = tokens.shape[-1]
    heads = row_decay.shape[1]
    doubled = row_select.shape[-1]
    half = doubled // 2
    width = model // heads
    flat = tokens.reshape(-1, model)
    T = flat.shape[0]
    fixed, parts = constants(
        T, heads, width, row_decay.shape[2], col_decay.shape[2], peers
    )
    strips = model // LANES
    tiles = 2 * strips * (half // PACK)
    vmem = pl.BlockSpec(memory_space=pltpu.VMEM)
    share = T // peers * parts
    operands = (
        flat,
        row_select.reshape(-1, doubled),
        row_decay.reshape(row_decay.shape[1:]),
        row_gain.reshape(1, -1),
        row_skip.reshape(1, -1),
        row_in,
        row_out,
        col_select.reshape(-1, doubled),
        col_decay.reshape(col_decay.shape[1:]),
        col_gain.reshape(1, -1),
        col_skip.reshape(1, -1),
        col_in,
        col_out,
        cotangent.reshape(-1, model),
    ) + fixed
    out = jax.ShapeDtypeStruct((T, model), BF16)
    mixed, grad = pl.pallas_call(
        functools.partial(kernel, (peers, frames, heads, width, parts)),
        out_shape=(out, out),
        in_specs=[pl.BlockSpec(memory_space=pltpu.HBM)] * len(operands),
        out_specs=(vmem, vmem),
        scratch_shapes=[pltpu.VMEM(a.shape, a.dtype) for a in operands]
        + [
            pltpu.SemaphoreType.DMA((len(operands),)),
            pltpu.VMEM((2, T, model), F32),
            pltpu.VMEM((2, T, model), F32),
            pltpu.VMEM((2, T, model), F32),
            pltpu.VMEM((strips, 2, LANES), F32),
            pltpu.VMEM((frames, peers, 2, LANES), F32),
            pltpu.VMEM((2, tiles, PACK, LANES), BF16),
            pltpu.VMEM((2, frames, peers, PACK, LANES), BF16),
            pltpu.VMEM((2, peers, PACK, LANES), BF16),
            pltpu.VMEM((2, tiles, PACK, LANES), BF16),
            pltpu.VMEM((2, peers, share, model // parts), BF16),
            pltpu.VMEM((2, peers, share, model // parts), BF16),
            pltpu.SemaphoreType.DMA((11,)),
            pltpu.SemaphoreType.DMA((11,)),
            pltpu.SemaphoreType.DMA((3, frames)),
        ],
        compiler_params=pltpu.CompilerParams(
            collective_id=0, has_side_effects=True, vmem_limit_bytes=62 * 1024 * 1024
        ),
    )(*operands)
    return (mixed.reshape(cotangent.shape), grad.reshape(tokens.shape))


def solution(mesh):
    token, decay = P("frame", "seq", None, None), P("frame", None, "seq", None)
    mixer = (token, decay, P(), P(), P(), P())
    return jax.shard_map(
        functools.partial(body, mesh.shape["seq"], mesh.shape["frame"]),
        mesh=mesh,
        in_specs=(token,) + mixer + mixer + (token,),
        out_specs=(token, token),
        check_vma=False,
    )
```
